1024 devices in a mesh: row: 32 (over z), col: 8 (over y, core), rep: 4 (over x).
Axes of the slice: x: 4, y: 4, z: 32, core: 2. Of those that a mesh axis runs over, the one named last changes fastest.
Arguments:
- density: bfloat16 [4096, 4096], P('row', 'col'), as said below
- block_mask: int32 [32, 32], replicated, may hold values from 0 to 1, as said below
- tile_order: int32 [32], replicated, may hold values from 0 to 31, as said below
Outputs:
- purified: bfloat16 [4096, 4096], P('row', 'col')
The draws below stay inside these ranges and needn't reach their ends.
Inputs may be any that keep to these rules, and one draw needn't show every extreme that they name: `block_mask`: symmetric; ones on the diagonal and wherever the two block indices lie within 2 of each other around a circle of 32. `tile_order`: a permutation of the block indices. `density`: symmetric, and zero outside the blocks that block_mask keeps, read in stored order.
All inputs are finite; a program needn't handle non-finite values.
Results may differ from the reference program's by a relative error of at most 0.0041.
Values may be sent and summed in bfloat16 or wider, within the bound.
No kernel may reach another device: no remote copies, remote signals or barrier semaphores. Data moves between devices by JAX's collectives and lax.ppermute only.
A program may use at most 32 MiB of HBM per device.

```python
import jax
import jax.numpy as jnp

TILE = 128
STEPS = 2
NB = 32


def shared_blocks(key):
    mask_key = jax.random.fold_in(key, 101)
    order_key = jax.random.fold_in(key, 102)
    blocks = NB
    index = jnp.arange(blocks, dtype=jnp.int32)
    apart = jnp.abs(index[:, None] - index[None, :])
    beside_all = jnp.minimum(apart, blocks - apart)
    extra = jax.random.randint(mask_key, (blocks, blocks), 0, 16, dtype=jnp.int32)
    upper = jnp.where((extra == 0) & (index[:, None] < index[None, :]), 1, 0)
    linked = jnp.maximum(upper, upper.T)
    mask = jnp.where(beside_all <= 2, 1, linked).astype(jnp.int32)
    order = jax.random.permutation(order_key, blocks).astype(jnp.int32)
    return (mask, order)


def draw_block_mask(key, part):
    mask, order = shared_blocks(key)
    return mask


def draw_tile_order(key, part):
    mask, order = shared_blocks(key)
    return order


def draw_density(key, part):
    mask, order = shared_blocks(key)
    key = jax.random.fold_in(key, 7)
    noise_key, sign_key, size_key = jax.random.split(key, 3)
    stored = mask[order][:, order].astype(jnp.float32)
    blocks = NB
    order_n = blocks * TILE
    retain = jnp.broadcast_to(stored[:, None, :, None], (blocks, TILE, blocks, TILE)).reshape(order_n, order_n)
    scale = 0.5 / (8.0 * TILE) ** 0.5
    noise = jax.random.normal(noise_key, (order_n, order_n), jnp.float32)
    sizes = jax.random.uniform(size_key, (order_n,), jnp.float32, 0.3, 0.9)
    signs = jnp.where(jax.random.randint(sign_key, (order_n,), 0, 2) == 0, -1.0, 1.0)
    symmetric = (noise + noise.T) * 0.7071
    index = jnp.arange(order_n)
    diagonal = jnp.where(index[:, None] == index[None, :], (signs * sizes)[:, None], 0.0)
    offdiag = jnp.where(index[:, None] == index[None, :], 0.0, retain * symmetric * scale)
    return (offdiag + diagonal).astype(jnp.bfloat16)


def setup_inputs(seed: int = 0) -> dict:
    key_of = jax.random.split(jax.random.key(seed), 4)
    density = draw_density(jax.random.fold_in(key_of[3], 71), 0)
    block_mask = draw_block_mask(jax.random.fold_in(key_of[3], 71), 0)
    tile_order = draw_tile_order(jax.random.fold_in(key_of[3], 71), 0)
    return {"density": density, "block_mask": block_mask, "tile_order": tile_order}


def reference(density, block_mask, tile_order):
    stored = block_mask[tile_order][:, tile_order].astype(jnp.float32)
    blocks = stored.shape[0]
    retain = jnp.broadcast_to(stored[:, None, :, None], (blocks, TILE, blocks, TILE)).reshape(blocks * TILE, blocks * TILE)
    matrix = density
    for step_number in range(STEPS):
        square = jnp.dot(matrix, matrix, preferred_element_type=jnp.float32)
        filtered = (retain * square).astype(jnp.bfloat16)
        cube = jnp.dot(matrix, filtered, preferred_element_type=jnp.float32)
        matrix = (retain * (1.5 * matrix.astype(jnp.float32) - 0.5 * cube)).astype(jnp.bfloat16)
    return matrix
```

```python
import jax
import jax.numpy as jnp
from jax import lax
from jax.experimental import pallas as pl
from jax.experimental.pallas import tpu as pltpu
from jax.sharding import PartitionSpec as P

TILE = 128
STEPS = 2
CHUNK = 16
CLASSES = 4
PER_ROW = 3
CLASS_CAP = 44
HALF = CLASSES * CLASS_CAP
NEAR = 16
GROUP = 8
ZERO = 2 * HALF


def dense(density, stored):
    height, breadth = density.shape
    layer_count = lax.axis_size("rep")
    layer_index = lax.axis_index("rep")
    row_count = lax.axis_size("row")
    row_index = lax.axis_index("row")
    col_index = lax.axis_index("col")
    block_rows = height // TILE
    block_cols = breadth // TILE
    local_blocks = lax.dynamic_slice(
        stored, (row_index * block_rows, col_index * block_cols), (block_rows, block_cols)
    )
    retain = jnp.broadcast_to(
        local_blocks[:, None, :, None], (block_rows, TILE, block_cols, TILE)
    ).reshape(height, breadth)

    def multiply(gathered_panel, operand):
        sub_rows = height // layer_count
        shaped = gathered_panel.reshape(height, row_count, layer_count, sub_rows)
        selected = lax.dynamic_index_in_dim(shaped, layer_index, 2, keepdims=False).reshape(
            height, row_count * sub_rows
        )
        portion_rows = lax.dynamic_slice_in_dim(operand, layer_index * sub_rows, sub_rows, 0)
        partial_sum = jnp.dot(
            selected,
            lax.all_gather(portion_rows, "row", axis=0, tiled=True),
            preferred_element_type=jnp.float32,
        )
        return lax.psum(partial_sum, "rep")

    matrix = density
    for step_number in range(STEPS):
        gathered_panel = lax.all_gather(matrix, "col", axis=1, tiled=True)
        square = multiply(gathered_panel, matrix)
        filtered = (retain * square).astype(jnp.bfloat16)
        cube = multiply(gathered_panel, filtered)
        matrix = (retain * (1.5 * matrix.astype(jnp.float32) - 0.5 * cube)).astype(jnp.bfloat16)
    return matrix


def exact_dot(a, b):
    return jnp.dot(
        a.astype(jnp.bfloat16), b.astype(jnp.bfloat16), preferred_element_type=jnp.float32
    )


def tables(stored, tile_order, row, col, rep):
    nb = stored.shape[0]
    kept = stored > 0.5
    index = jnp.arange(nb, dtype=jnp.int32)
    before = (index[:, None] < index[None, :]).astype(jnp.float32)
    apart = (tile_order[None, :] - tile_order[:, None]) % nb
    mine = (apart < nb // 2) | ((apart == nb // 2) & (tile_order[:, None] < nb // 2))
    own = (kept & mine).astype(jnp.float32)
    rank = exact_dot(own, before).astype(jnp.int32)
    owned = jnp.sum(own, axis=1).astype(jnp.int32)
    classes = jnp.arange(CLASSES, dtype=jnp.int32)
    first = (classes[:, None] - index[None, :]) % CLASSES
    count = (owned[None, :] - first + CLASSES - 1) // CLASSES
    base = jnp.sum(
        jnp.where(index[None, None, :] < index[None, :, None], count[:, None, :], 0), axis=2
    )
    total = jnp.sum(count, axis=1)
    wanted = jnp.arange(PER_ROW, dtype=jnp.int32) * CLASSES + (rep - row) % CLASSES
    row_own = lax.dynamic_index_in_dim(own, row, 0, keepdims=False) > 0.5
    row_rank = lax.dynamic_index_in_dim(rank, row, 0, keepdims=False)
    hit = row_own[None, :] & (row_rank[None, :] == wanted[:, None])
    send = jnp.sum(jnp.where(hit, index[None, :] + 1, 0), axis=1) - 1
    my_base = lax.dynamic_index_in_dim(base, rep, 0, keepdims=False)
    my_count = lax.dynamic_index_in_dim(count, rep, 0, keepdims=False)
    place = jnp.arange(CLASS_CAP, dtype=jnp.int32)[:, None]
    inside = (place >= my_base[None, :]) & (place < (my_base + my_count)[None, :])
    keep = (
        jnp.sum(
            jnp.where(inside, index[None, :] * PER_ROW + place - my_base[None, :] + 1, 0), axis=1
        )
        - 1
    )
    which = (rank + index[:, None]) % CLASSES
    start = jnp.zeros_like(rank)
    for c in range(CLASSES):
        start = jnp.where(which == c, base[c][:, None] + c * CLASS_CAP, start)
    slot = start + rank // CLASSES
    slots = jnp.where(own > 0.5, slot, jnp.where(kept, slot.T + HALF, ZERO))
    a = stored
    er = lax.dynamic_index_in_dim(stored, row, 0, keepdims=False)
    k_set = er * ((index // (nb // 8)) == col)
    through = exact_dot(a * k_set[None, :], a)
    need_x = kept & ((k_set[None, :] > 0.5) | ((er[:, None] > 0.5) & (through > 0.5)))
    need_f = kept & (exact_dot(a, need_x) > 0.5)
    x_slots = jnp.where(need_x, slots, ZERO)
    f_slots = jnp.where(need_f, slots, ZERO)
    pad = lambda t: jnp.pad(t, ((0, 1), (0, 1)), constant_values=ZERO)
    near_rank = exact_dot(a, before).astype(jnp.int32)
    steps = jnp.arange(NEAR, dtype=jnp.int32)
    near_hit = kept[:, None, :] & (near_rank[:, None, :] == steps[None, :, None])
    near = jnp.sum(jnp.where(near_hit, index[None, None, :] - nb, 0), axis=2) + nb
    near_count = jnp.sum(kept.astype(jnp.int32), axis=1)
    fits = (
        (jnp.max(owned) <= PER_ROW * CLASSES)
        & (jnp.max(total) <= CLASS_CAP)
        & (jnp.max(near_count) <= NEAR)
    )
    return fits, dict(
        send=send,
        keep=keep,
        slots=pad(slots),
        x_slots=pad(x_slots),
        f_slots=pad(f_slots),
        near=near,
        near_count=near_count,
        total=total,
    )


def pick_kernel(send_ref, got_ref, out_ref):
    for t in range(PER_ROW):
        b = send_ref[t]
        at = jnp.maximum(b, 0)
        tile = got_ref[at // 4, :, pl.ds(pl.multiple_of((at % 4) * TILE, TILE), TILE)]
        out_ref[t] = jnp.where(b >= 0, tile, jnp.zeros_like(tile))


def pack_kernel(keep_ref, all_ref, out_ref):
    def one(p, carry):
        e = keep_ref[p]
        tile = all_ref[jnp.maximum(e, 0)]
        out_ref[p] = jnp.where(e >= 0, tile, jnp.zeros_like(tile))
        return carry

    lax.fori_loop(0, CLASS_CAP, one, 0, unroll=4)


def purify_kernel(
    place_ref,
    total_ref,
    slots_ref,
    x_slots_ref,
    f_slots_ref,
    near_ref,
    near_count_ref,
    own_ref,
    other_ref,
    out_ref,
    w,
    f,
    x,
    sems,
):
    row, col, core = place_ref[0], place_ref[1], place_ref[2]
    nb = 32

    def copies():
        for part, (ref, half) in enumerate(((own_ref, core), (other_ref, 1 - core))):
            for q in range(CLASSES):
                for y in range(4):
                    yield pltpu.make_async_copy(
                        ref.at[q * 4 + y],
                        w.at[pl.ds(q * CLASS_CAP, CLASS_CAP), 2 * y + half],
                        sems.at[part * 16 + q * 4 + y],
                    )

    for c in copies():
        c.start()
    zero = jnp.zeros((TILE, TILE), jnp.bfloat16)
    w[ZERO] = zero.reshape(8, CHUNK, TILE)
    f[ZERO] = zero
    x[ZERO] = zero
    for c in copies():
        c.wait()

    def w_at(s):
        return w[s].reshape(TILE, TILE)

    for q in range(CLASSES):

        def turn(p, carry, q=q):
            s = q * CLASS_CAP + p
            w[s + HALF] = w_at(s).T.reshape(8, CHUNK, TILE)
            return carry

        lax.fori_loop(0, total_ref[q], turn, 0)

    def product(i, j, left, left_slots, right, right_slots):
        def some(g):
            ls = [near_ref[j, g * GROUP + t] for t in range(GROUP)]
            lhs = jnp.concatenate([left(left_slots[i, l]) for l in ls], axis=1)
            rhs = jnp.concatenate([right(right_slots[l, j]) for l in ls], axis=0)
            return jnp.dot(lhs, rhs, preferred_element_type=jnp.float32)

        return lax.cond(
            near_count_ref[j] > GROUP, lambda: some(0) + some(1), lambda: some(0)
        )

    f_at = lambda s: f[s]
    x_at = lambda s: x[s]

    def f_column(j, carry):
        def one(t, carry):
            i = near_ref[j, t]
            s = f_slots_ref[i, j]

            @pl.when(s != ZERO)
            def _():
                f[s] = product(i, j, w_at, slots_ref, w_at, slots_ref).astype(jnp.bfloat16)

            return carry

        return lax.fori_loop(0, near_count_ref[j], one, carry)

    lax.fori_loop(0, nb, f_column, 0)

    def x_column(j, carry):
        def one(t, carry):
            i = near_ref[j, t]
            s = x_slots_ref[i, j]

            @pl.when(s != ZERO)
            def _():
                cube = product(i, j, w_at, slots_ref, f_at, f_slots_ref)
                x[s] = (1.5 * w_at(s).astype(jnp.float32) - 0.5 * cube).astype(jnp.bfloat16)

            return carry

        return lax.fori_loop(0, near_count_ref[j], one, carry)

    lax.fori_loop(0, nb, x_column, 0)

    for b in range(4):
        k = col * 4 + b
        own = slots_ref[row, k]

        def one(t, total, k=k):
            m = near_ref[k, t]

            def add():
                square = product(m, k, x_at, x_slots_ref, x_at, x_slots_ref).astype(jnp.bfloat16)
                return total + jnp.dot(
                    x[x_slots_ref[row, m]], square, preferred_element_type=jnp.float32
                )

            return lax.cond(slots_ref[row, m] != ZERO, add, lambda: total)

        trips = jnp.where(own != ZERO, near_count_ref[k], 0)
        cube = lax.fori_loop(0, trips, one, jnp.zeros((TILE, TILE), jnp.float32))
        mine = jnp.where(own != ZERO, x_slots_ref[row, k], ZERO)
        out_ref[:, b * TILE : (b + 1) * TILE] = (
            1.5 * x[mine].astype(jnp.float32) - 0.5 * cube
        ).astype(jnp.bfloat16)


SMEM = pl.BlockSpec(memory_space=pltpu.SMEM)
VMEM = pl.BlockSpec(memory_space=pltpu.VMEM)
ANY = pl.BlockSpec(memory_space=pl.ANY)


def sparse(density, table, row, col, rep):
    bf16 = jnp.bfloat16
    rows = lax.axis_size("row")
    got = lax.all_to_all(density.reshape(8, CHUNK, 4 * TILE), "col", 0, 0)
    picked = pl.pallas_call(
        pick_kernel,
        out_shape=jax.ShapeDtypeStruct((PER_ROW, CHUNK, TILE), bf16),
        in_specs=[SMEM, VMEM],
        out_specs=VMEM,
    )(table["send"], got)
    everywhere = lax.all_gather(picked, "row", axis=0, tiled=True)
    packed = pl.pallas_call(
        pack_kernel,
        out_shape=jax.ShapeDtypeStruct((CLASS_CAP, CHUNK, TILE), bf16),
        in_specs=[SMEM, VMEM],
        out_specs=VMEM,
    )(table["keep"], everywhere)
    groups = [[q * 8 + c for q in range(4) for c in range(k, 8, 2)] for k in (0, 1)]
    own = lax.all_to_all(
        jnp.broadcast_to(packed[None], (16,) + packed.shape),
        ("rep", "col"),
        0,
        0,
        axis_index_groups=groups,
    )
    other = lax.ppermute(own, "col", [(i, i ^ 1) for i in range(8)])
    place = jnp.stack([row, col, col % 2]).astype(jnp.int32)
    return pl.pallas_call(
        purify_kernel,
        out_shape=jax.ShapeDtypeStruct((TILE, 4 * TILE), bf16),
        in_specs=[SMEM] * 7 + [ANY, ANY],
        out_specs=VMEM,
        scratch_shapes=[
            pltpu.VMEM((ZERO + 1, 8, CHUNK, TILE), bf16),
            pltpu.VMEM((ZERO + 1, TILE, TILE), bf16),
            pltpu.VMEM((ZERO + 1, TILE, TILE), bf16),
            pltpu.SemaphoreType.DMA((32,)),
        ],
        compiler_params=pltpu.CompilerParams(vmem_limit_bytes=44 * 1024 * 1024),
    )(
        place,
        table["total"],
        table["slots"],
        table["x_slots"],
        table["f_slots"],
        table["near"],
        table["near_count"],
        own,
        other,
    )


def body(density, block_mask, tile_order):
    row, col, rep = (lax.axis_index(a) for a in ("row", "col", "rep"))
    blocks = block_mask.shape[0]
    onehot = (tile_order[:, None] == jnp.arange(blocks, dtype=jnp.int32)[None, :]).astype(
        jnp.float32
    )
    stored = exact_dot(exact_dot(onehot, block_mask), onehot.T)
    fits, table = tables(stored, tile_order, row, col, rep)
    return lax.cond(
        fits,
        lambda: sparse(density, table, row, col, rep),
        lambda: dense(density, stored),
    )


def solution(mesh):
    return jax.shard_map(
        body,
        mesh=mesh,
        in_specs=(P("row", "col"), P(), P()),
        out_specs=P("row", "col"),
        check_vma=False,
    )
```

```python
import jax
import jax.numpy as jnp
from jax import lax
from jax.experimental import pallas as pl
from jax.experimental.pallas import tpu as pltpu
from jax.sharding import PartitionSpec as P

TILE = 128
STEPS = 2
CHUNK = 16
CLASSES = 4
PER_ROW = 3
CLASS_CAP = 40
HALF = CLASSES * CLASS_CAP
GROUP = 4
PAIRS = 6
TURN = 10
ZERO = 2 * HALF


def dense(density, stored):
    height, breadth = density.shape
    layer_count = lax.axis_size("rep")
    layer_index = lax.axis_index("rep")
    row_count = lax.axis_size("row")
    row_index = lax.axis_index("row")
    col_index = lax.axis_index("col")
    block_rows = height // TILE
    block_cols = breadth // TILE
    local_blocks = lax.dynamic_slice(
        stored, (row_index * block_rows, col_index * block_cols), (block_rows, block_cols)
    )
    retain = jnp.broadcast_to(
        local_blocks[:, None, :, None], (block_rows, TILE, block_cols, TILE)
    ).reshape(height, breadth)

    def multiply(gathered_panel, operand):
        sub_rows = height // layer_count
        shaped = gathered_panel.reshape(height, row_count, layer_count, sub_rows)
        selected = lax.dynamic_index_in_dim(shaped, layer_index, 2, keepdims=False).reshape(
            height, row_count * sub_rows
        )
        portion_rows = lax.dynamic_slice_in_dim(operand, layer_index * sub_rows, sub_rows, 0)
        partial_sum = jnp.dot(
            selected,
            lax.all_gather(portion_rows, "row", axis=0, tiled=True),
            preferred_element_type=jnp.float32,
        )
        return lax.psum(partial_sum, "rep")

    matrix = density
    for step_number in range(STEPS):
        gathered_panel = lax.all_gather(matrix, "col", axis=1, tiled=True)
        square = multiply(gathered_panel, matrix)
        filtered = (retain * square).astype(jnp.bfloat16)
        cube = multiply(gathered_panel, filtered)
        matrix = (retain * (1.5 * matrix.astype(jnp.float32) - 0.5 * cube)).astype(jnp.bfloat16)
    return matrix


def exact_dot(a, b):
    return jnp.dot(
        a.astype(jnp.bfloat16), b.astype(jnp.bfloat16), preferred_element_type=jnp.float32
    )


def owners(stored, tile_order):
    nb = stored.shape[0]
    index = jnp.arange(nb, dtype=jnp.int32)
    apart = (tile_order[None, :] - tile_order[:, None]) % nb
    mine = (apart < nb // 2) | ((apart == nb // 2) & (tile_order[:, None] < nb // 2))
    own = jnp.where(mine, stored, 0)
    owned = jnp.sum(own, axis=1).astype(jnp.int32)
    classes = jnp.arange(CLASSES, dtype=jnp.int32)
    first = (classes[:, None] - index[None, :]) % CLASSES
    count = (owned[None, :] - first + CLASSES - 1) // CLASSES
    total = jnp.sum(count, axis=1)
    over = jnp.concatenate([owned - PER_ROW * CLASSES, total - CLASS_CAP])
    return own, count, jnp.max(over) <= 0


def tables(stored, own, count, row, col, rep):
    nb = stored.shape[0]
    kept = stored > 0.5
    index = jnp.arange(nb, dtype=jnp.int32)
    before = (index[:, None] < index[None, :]).astype(jnp.float32)
    rank = exact_dot(own, before).astype(jnp.int32)
    total = jnp.sum(count, axis=1)
    base = jnp.sum(
        jnp.where(index[None, None, :] < index[None, :, None], count[:, None, :], 0), axis=2
    )
    wanted = jnp.arange(PER_ROW, dtype=jnp.int32) * CLASSES + (rep - row) % CLASSES
    row_own = lax.dynamic_index_in_dim(own, row, 0, keepdims=False) > 0.5
    row_rank = lax.dynamic_index_in_dim(rank, row, 0, keepdims=False)
    hit = row_own[None, :] & (row_rank[None, :] == wanted[:, None])
    send = jnp.sum(jnp.where(hit, index[None, :] + 1, 0), axis=1) - 1
    my_base = lax.dynamic_index_in_dim(base, rep, 0, keepdims=False)
    my_count = lax.dynamic_index_in_dim(count, rep, 0, keepdims=False)
    place = jnp.arange(CLASS_CAP, dtype=jnp.int32)[:, None]
    inside = (place >= my_base[None, :]) & (place < (my_base + my_count)[None, :])
    arrived = index ^ (row % 2)
    keep = (
        jnp.sum(
            jnp.where(inside, arrived[None, :] * PER_ROW + place - my_base[None, :] + 1, 0), axis=1
        )
        - 1
    )
    which = (rank + index[:, None]) % CLASSES
    start = jnp.zeros_like(rank)
    for c in range(CLASSES):
        start = jnp.where(which == c, base[c][:, None] + c * CLASS_CAP, start)
    slot = start + rank // CLASSES
    slots = jnp.where(own > 0.5, slot, jnp.where(kept, slot.T + HALF, ZERO))
    a = stored
    er = lax.dynamic_index_in_dim(stored, row, 0, keepdims=False)
    k_set = er * ((index // (nb // 8)) == col)
    through = exact_dot(a * k_set[None, :], a)
    need_x = kept & ((k_set[None, :] > 0.5) | ((er[:, None] > 0.5) & (through > 0.5)))
    need_f = exact_dot(a, need_x) > 0.5
    need_f = kept & (need_f | need_f.T)
    x_slots = jnp.where(need_x, slots, ZERO)
    f_slots = jnp.where(need_f, slots, ZERO)
    pad = lambda t: jnp.pad(t, ((1, 0), (1, 0)), constant_values=ZERO)
    powers = jnp.left_shift(jnp.int32(1), index)
    bits = lambda t: jnp.pad(jnp.sum(jnp.where(t, powers[:, None], 0), axis=0), (1, 0))
    chunks = (exact_dot(a, a).astype(jnp.int32) + GROUP - 1) // GROUP
    return dict(
        send=send,
        keep=keep,
        slots=pad(slots),
        x_slots=pad(x_slots),
        f_slots=pad(f_slots),
        count=jnp.pad(chunks, ((1, 0), (1, 0))),
        near=bits(kept),
        f_bits=bits(need_f & (own > 0.5)),
        x_bits=bits(need_x),
        total=total,
    )


def pick_kernel(send_ref, got_ref, out_ref):
    for t in range(PER_ROW):
        b = send_ref[t]
        at = jnp.maximum(b, 0)
        tile = got_ref[at // 4, :, pl.ds(pl.multiple_of((at % 4) * TILE, TILE), TILE)]
        out_ref[t] = jnp.where(b >= 0, tile, jnp.zeros_like(tile))


def pack_kernel(keep_ref, all_ref, out_ref):
    def one(p, carry):
        e = keep_ref[p]
        tile = all_ref[jnp.maximum(e, 0)]
        out_ref[p] = jnp.where(e >= 0, tile, jnp.zeros_like(tile))
        return carry

    lax.fori_loop(0, CLASS_CAP, one, 0, unroll=4)


def purify_kernel(
    place_ref,
    total_ref,
    slots_ref,
    x_slots_ref,
    f_slots_ref,
    count_ref,
    near_ref,
    f_bits_ref,
    x_bits_ref,
    own_ref,
    other_ref,
    out_ref,
    w,
    f,
    x,
    todo,
    length,
    sems,
):
    row, col, core = place_ref[0], place_ref[1], place_ref[2]
    nb = 32

    def copies():
        for part, (ref, half) in enumerate(((own_ref, core), (other_ref, 1 - core))):
            for q in range(CLASSES):
                for y in range(4):
                    yield pltpu.make_async_copy(
                        ref.at[q * 4 + y],
                        w.at[pl.ds(q * CLASS_CAP, CLASS_CAP), 2 * y + half],
                        sems.at[part * 16 + q * 4 + y],
                    )

    for c in copies():
        c.start()
    zero = jnp.zeros((TILE, TILE), jnp.bfloat16)
    w[ZERO] = zero.reshape(8, CHUNK, TILE)
    f[ZERO] = zero
    x[ZERO] = zero
    def lowest(bits):
        return 32 - lax.clz(bits & -bits), bits & (bits - 1)

    for part, bits_ref in enumerate((f_bits_ref, x_bits_ref)):
        length[part, 0] = 0
        length[part, 1] = 0

        def column(j, carry, part=part, bits_ref=bits_ref):
            def add(bits):
                i, bits = lowest(bits)
                heavy = (count_ref[i, j] > 1).astype(jnp.int32)
                at = length[part, heavy]
                todo[part, heavy, at] = i * 64 + j
                length[part, heavy] = at + 1
                return bits

            lax.while_loop(lambda bits: bits != 0, add, bits_ref[j])
            return carry

        lax.fori_loop(1, nb + 1, column, 0)
        for heavy in (0, 1):
            for u in range(PAIRS):
                todo[part, heavy, length[part, heavy] + u] = 0

    for c in copies():
        c.wait()

    w_at = lambda s: w[s].reshape(TILE, TILE)
    f_at = lambda s: f[s]
    x_at = lambda s: x[s]

    for q in range(CLASSES):

        def turn(p, carry, q=q):
            for u in range(TURN):
                s = q * CLASS_CAP + p * TURN + u
                w[s + HALF] = w_at(s).T.reshape(8, CHUNK, TILE)
            return carry

        lax.fori_loop(0, (total_ref[q] + TURN - 1) // TURN, turn, 0)

    def product(pairs, chunks, left, left_slots, right, right_slots):
        def some(state):
            sums, masks = [], []
            for (i, j), bits in zip(pairs, state):
                lhs, rhs = [], []
                for _ in range(GROUP):
                    l, bits = lowest(bits)
                    lhs.append(left(left_slots[i, l]))
                    rhs.append(right(right_slots[l, j]))
                sums.append(
                    jnp.dot(
                        jnp.concatenate(lhs, axis=1),
                        jnp.concatenate(rhs, axis=0),
                        preferred_element_type=jnp.float32,
                    )
                )
                masks.append(bits)
            return sums, masks

        masks = [near_ref[i] & near_ref[j] for i, j in pairs]
        sums, masks = some(masks)
        if chunks is None:
            return sums

        def more(_, state):
            sums, masks = state
            extra, masks = some(masks)
            return [u + v for u, v in zip(sums, extra)], masks

        sums, _ = lax.fori_loop(1, chunks, more, (sums, masks))
        return sums

    def listed(part, work):
        for heavy in (0, 1):

            def some(g, carry, heavy=heavy):
                pairs = []
                for u in range(PAIRS):
                    code = todo[part, heavy, g * PAIRS + u]
                    pairs.append((code >> 6, code & 63))
                chunks = None
                if heavy:
                    chunks = most(pairs)
                work(pairs, chunks)
                return carry

            lax.fori_loop(0, (length[part, heavy] + PAIRS - 1) // PAIRS, some, 0)

    def most(pairs):
        chunks = count_ref[pairs[0][0], pairs[0][1]]
        for i, j in pairs[1:]:
            chunks = jnp.maximum(chunks, count_ref[i, j])
        return chunks

    def f_work(pairs, chunks):
        for (i, j), total in zip(pairs, product(pairs, chunks, w_at, slots_ref, w_at, slots_ref)):
            block = total.astype(jnp.bfloat16)
            f[slots_ref[i, j]] = block
            f[slots_ref[j, i]] = block.T

    def x_work(pairs, chunks):
        for (i, j), cube in zip(pairs, product(pairs, chunks, w_at, slots_ref, f_at, f_slots_ref)):
            s = x_slots_ref[i, j]
            x[s] = (1.5 * w_at(s).astype(jnp.float32) - 0.5 * cube).astype(jnp.bfloat16)

    listed(0, f_work)
    listed(1, x_work)

    for b in range(4):
        k = col * 4 + b + 1
        mine = x_slots_ref[row + 1, k]

        def some(state, k=k):
            total, bits = state
            pairs = []
            for _ in range(PAIRS):
                m, bits = lowest(bits)
                pairs.append((m, k))
            squares = product(pairs, most(pairs), x_at, x_slots_ref, x_at, x_slots_ref)
            lhs = jnp.concatenate([x[x_slots_ref[row + 1, m]] for m, _ in pairs], axis=1)
            rhs = jnp.concatenate([v.astype(jnp.bfloat16) for v in squares], axis=0)
            return total + jnp.dot(lhs, rhs, preferred_element_type=jnp.float32), bits

        bits = jnp.where(slots_ref[row + 1, k] != ZERO, near_ref[row + 1] & near_ref[k], 0)
        cube, _ = lax.while_loop(
            lambda state: state[1] != 0, some, (jnp.zeros((TILE, TILE), jnp.float32), bits)
        )
        mine = jnp.where(slots_ref[row + 1, k] != ZERO, mine, ZERO)
        out_ref[:, b * TILE : (b + 1) * TILE] = (
            1.5 * x[mine].astype(jnp.float32) - 0.5 * cube
        ).astype(jnp.bfloat16)


SMEM = pl.BlockSpec(memory_space=pltpu.SMEM)
VMEM = pl.BlockSpec(memory_space=pltpu.VMEM)
ANY = pl.BlockSpec(memory_space=pl.ANY)


def run_purify(own, other, place, table):
    bf16 = jnp.bfloat16
    return pl.pallas_call(
        purify_kernel,
        out_shape=jax.ShapeDtypeStruct((TILE, 4 * TILE), bf16),
        in_specs=[SMEM] * 9 + [ANY, ANY],
        out_specs=VMEM,
        scratch_shapes=[
            pltpu.VMEM((ZERO + 1, 8, CHUNK, TILE), bf16),
            pltpu.VMEM((ZERO + 1, TILE, TILE), bf16),
            pltpu.VMEM((ZERO + 1, TILE, TILE), bf16),
            pltpu.SMEM((2, 2, 1152), jnp.int32),
            pltpu.SMEM((2, 2), jnp.int32),
            pltpu.SemaphoreType.DMA((32,)),
        ],
        compiler_params=pltpu.CompilerParams(vmem_limit_bytes=44 * 1024 * 1024),
    )(
        place,
        table["total"],
        table["slots"],
        table["x_slots"],
        table["f_slots"],
        table["count"],
        table["near"],
        table["f_bits"],
        table["x_bits"],
        own,
        other,
    )


def sparse(density, table, row, col, rep):
    bf16 = jnp.bfloat16
    rows = lax.axis_size("row")
    got = lax.all_to_all(density.reshape(8, CHUNK, 4 * TILE), "col", 0, 0)
    picked = pl.pallas_call(
        pick_kernel,
        out_shape=jax.ShapeDtypeStruct((PER_ROW, CHUNK, TILE), bf16),
        in_specs=[SMEM, VMEM],
        out_specs=VMEM,
    )(table["send"], got)
    swapped = lax.ppermute(picked, "row", [(i, i ^ 1) for i in range(rows)])
    everywhere = lax.all_gather(
        jnp.stack([picked, swapped]),
        "row",
        axis_index_groups=[list(range(i, rows, 2)) for i in range(2)],
    ).reshape(rows * PER_ROW, CHUNK, TILE)
    packed = pl.pallas_call(
        pack_kernel,
        out_shape=jax.ShapeDtypeStruct((CLASS_CAP, CHUNK, TILE), bf16),
        in_specs=[SMEM, VMEM],
        out_specs=VMEM,
    )(table["keep"], everywhere)
    groups = [[q * 8 + c for q in range(4) for c in range(k, 8, 2)] for k in (0, 1)]
    own = lax.all_to_all(
        jnp.broadcast_to(packed[None], (16,) + packed.shape),
        ("rep", "col"),
        0,
        0,
        axis_index_groups=groups,
    )
    other = lax.ppermute(own, "col", [(i, i ^ 1) for i in range(8)])
    place = jnp.stack([row, col, col % 2]).astype(jnp.int32)
    return run_purify(own, other, place, table)


def body(density, block_mask, tile_order):
    row, col, rep = (lax.axis_index(a) for a in ("row", "col", "rep"))
    blocks = block_mask.shape[0]
    onehot = (tile_order[:, None] == jnp.arange(blocks, dtype=jnp.int32)[None, :]).astype(
        jnp.float32
    )
    stored = exact_dot(exact_dot(onehot, block_mask), onehot.T)
    own, count, fits = owners(stored, tile_order)
    return lax.cond(
        fits,
        lambda: sparse(density, tables(stored, own, count, row, col, rep), row, col, rep),
        lambda: dense(density, stored),
    )


def solution(mesh):
    return jax.shard_map(
        body,
        mesh=mesh,
        in_specs=(P("row", "col"), P(), P()),
        out_specs=P("row", "col"),
        check_vma=False,
    )
```

```python
import functools

import jax
import jax.numpy as jnp
from jax import lax
from jax.experimental import pallas as pl
from jax.experimental.pallas import tpu as pltpu
from jax.sharding import PartitionSpec as P

TILE = 128
STEPS = 2
CHUNK = 16
CLASSES = 4
PER_ROW = 3
CLASS_CAP = 40
HALF = CLASSES * CLASS_CAP
GROUPS = (4, 8, 8)
LONG = len(GROUPS) - 1
PAIRS = (8, 4, 1)
LAST = 3
TURN = 10
ZERO = 2 * HALF


def dense(density, stored):
    height, breadth = density.shape
    layer_count = lax.axis_size("rep")
    layer_index = lax.axis_index("rep")
    row_count = lax.axis_size("row")
    row_index = lax.axis_index("row")
    col_index = lax.axis_index("col")
    block_rows = height // TILE
    block_cols = breadth // TILE
    local_blocks = lax.dynamic_slice(
        stored, (row_index * block_rows, col_index * block_cols), (block_rows, block_cols)
    )
    retain = jnp.broadcast_to(
        local_blocks[:, None, :, None], (block_rows, TILE, block_cols, TILE)
    ).reshape(height, breadth)

    def multiply(gathered_panel, operand):
        sub_rows = height // layer_count
        shaped = gathered_panel.reshape(height, row_count, layer_count, sub_rows)
        selected = lax.dynamic_index_in_dim(shaped, layer_index, 2, keepdims=False).reshape(
            height, row_count * sub_rows
        )
        portion_rows = lax.dynamic_slice_in_dim(operand, layer_index * sub_rows, sub_rows, 0)
        partial_sum = jnp.dot(
            selected,
            lax.all_gather(portion_rows, "row", axis=0, tiled=True),
            preferred_element_type=jnp.float32,
        )
        return lax.psum(partial_sum, "rep")

    matrix = density
    for step_number in range(STEPS):
        gathered_panel = lax.all_gather(matrix, "col", axis=1, tiled=True)
        square = multiply(gathered_panel, matrix)
        filtered = (retain * square).astype(jnp.bfloat16)
        cube = multiply(gathered_panel, filtered)
        matrix = (retain * (1.5 * matrix.astype(jnp.float32) - 0.5 * cube)).astype(jnp.bfloat16)
    return matrix


def exact_dot(a, b):
    return jnp.dot(
        a.astype(jnp.bfloat16), b.astype(jnp.bfloat16), preferred_element_type=jnp.float32
    )


def owners(stored, tile_order):
    nb = stored.shape[0]
    index = jnp.arange(nb, dtype=jnp.int32)
    apart = (tile_order[None, :] - tile_order[:, None]) % nb
    mine = (apart < nb // 2) | ((apart == nb // 2) & (tile_order[:, None] < nb // 2))
    own = jnp.where(mine, stored, 0)
    owned = jnp.sum(own, axis=1).astype(jnp.int32)
    classes = jnp.arange(CLASSES, dtype=jnp.int32)
    first = (classes[:, None] - index[None, :]) % CLASSES
    count = (owned[None, :] - first + CLASSES - 1) // CLASSES
    total = jnp.sum(count, axis=1)
    over = jnp.concatenate([owned - PER_ROW * CLASSES, total - CLASS_CAP])
    return own, count, jnp.max(over) <= 0


def tables(stored, own, count, row, col, rep):
    nb = stored.shape[0]
    kept = stored > 0.5
    index = jnp.arange(nb, dtype=jnp.int32)
    before = (index[:, None] < index[None, :]).astype(jnp.float32)
    rank = exact_dot(own, before).astype(jnp.int32)
    total = jnp.sum(count, axis=1)
    base = jnp.sum(
        jnp.where(index[None, None, :] < index[None, :, None], count[:, None, :], 0), axis=2
    )
    pair = row - row % 2
    pair_own = lax.dynamic_slice_in_dim(own, pair, 2, 0) > 0.5
    pair_rank = lax.dynamic_slice_in_dim(rank, pair, 2, 0)
    turn = (rep - pair - jnp.arange(2, dtype=jnp.int32)) % CLASSES
    wanted = jnp.arange(PER_ROW, dtype=jnp.int32)[None, :] * CLASSES + turn[:, None]
    hit = pair_own[:, None, :] & (pair_rank[:, None, :] == wanted[:, :, None])
    send = jnp.sum(jnp.where(hit, index[None, None, :] + 1, 0), axis=2) - 1
    send = send.reshape(2 * PER_ROW)
    my_base = lax.dynamic_index_in_dim(base, rep, 0, keepdims=False)
    my_count = lax.dynamic_index_in_dim(count, rep, 0, keepdims=False)
    place = jnp.arange(CLASS_CAP, dtype=jnp.int32)[:, None]
    inside = (place >= my_base[None, :]) & (place < (my_base + my_count)[None, :])
    keep = (
        jnp.sum(
            jnp.where(inside, index[None, :] * PER_ROW + place - my_base[None, :] + 1, 0), axis=1
        )
        - 1
    )
    which = (rank + index[:, None]) % CLASSES
    start = jnp.zeros_like(rank)
    for c in range(CLASSES):
        start = jnp.where(which == c, base[c][:, None] + c * CLASS_CAP, start)
    slot = start + rank // CLASSES
    slots = jnp.where(own > 0.5, slot, jnp.where(kept, slot.T + HALF, ZERO))
    a = stored
    er = lax.dynamic_index_in_dim(stored, row, 0, keepdims=False)
    k_set = er * ((index // (nb // 8)) == col)
    through = exact_dot(a * k_set[None, :], a)
    need_x = kept & ((k_set[None, :] > 0.5) | ((er[:, None] > 0.5) & (through > 0.5)))
    need_f = exact_dot(a, need_x) > 0.5
    need_f = kept & (need_f | need_f.T)
    x_slots = jnp.where(need_x, slots, ZERO)
    f_slots = jnp.where(need_f, slots, ZERO)
    pad = lambda t: jnp.pad(t, ((1, 0), (1, 0)), constant_values=ZERO)
    powers = jnp.left_shift(jnp.int32(1), index)
    bits = lambda t: jnp.pad(jnp.sum(jnp.where(t, powers[:, None], 0), axis=0), (1, 0))
    common = exact_dot(a, a)
    kinds = sum((common > g).astype(jnp.int32) for g in GROUPS[:LONG])
    return dict(
        send=send,
        keep=keep,
        slots=pad(slots),
        x_slots=pad(x_slots),
        f_slots=pad(f_slots),
        count=jnp.pad(kinds, ((1, 0), (1, 0))),
        near=bits(kept),
        f_bits=bits(need_f & (own > 0.5)),
        x_bits=bits(need_x),
        total=total,
    )


def pick_kernel(send_ref, got_ref, out_ref):
    for t in range(2 * PER_ROW):
        b = send_ref[t]
        at = jnp.maximum(b, 0)
        tile = got_ref[t // PER_ROW * 8 + at // 4, :, pl.ds(pl.multiple_of((at % 4) * TILE, TILE), TILE)]
        out_ref[t] = jnp.where(b >= 0, tile, jnp.zeros_like(tile))


def pack_kernel(keep_ref, all_ref, out_ref):
    def one(p, carry):
        e = keep_ref[p]
        tile = all_ref[jnp.maximum(e, 0)]
        out_ref[p] = jnp.where(e >= 0, tile, jnp.zeros_like(tile))
        return carry

    lax.fori_loop(0, CLASS_CAP, one, 0, unroll=4)


def purify_kernel(
    place_ref,
    total_ref,
    slots_ref,
    x_slots_ref,
    f_slots_ref,
    count_ref,
    near_ref,
    f_bits_ref,
    x_bits_ref,
    own_ref,
    other_ref,
    out_ref,
    w,
    f,
    x,
    todo,
    length,
    sems,
):
    row, col, core = place_ref[0], place_ref[1], place_ref[2]
    nb = 32

    def copies():
        for part, (ref, half) in enumerate(((own_ref, core), (other_ref, 1 - core))):
            for q in range(CLASSES):
                for y in range(4):
                    yield pltpu.make_async_copy(
                        ref.at[q * 4 + y],
                        w.at[pl.ds(q * CLASS_CAP, CLASS_CAP), 2 * y + half],
                        sems.at[part * 16 + q * 4 + y],
                    )

    for c in copies():
        c.start()
    zero = jnp.zeros((TILE, TILE), jnp.bfloat16)
    w[ZERO] = zero.reshape(8, CHUNK, TILE)
    f[ZERO] = zero
    x[ZERO] = zero
    def lowest(bits):
        return 32 - lax.clz(bits & -bits), bits & (bits - 1)

    for part, bits_ref in enumerate((f_bits_ref, x_bits_ref)):
        for kind in range(LONG + 1):
            length[part, kind] = 0

        def column(j, carry, part=part, bits_ref=bits_ref):
            def add(bits):
                i, bits = lowest(bits)
                kind = count_ref[i, j]
                at = length[part, kind]
                todo[part, kind, at] = i * 64 + j
                length[part, kind] = at + 1
                return bits

            lax.while_loop(lambda bits: bits != 0, add, bits_ref[j])
            return carry

        lax.fori_loop(1, nb + 1, column, 0)
        for kind in range(LONG + 1):
            for u in range(PAIRS[kind]):
                todo[part, kind, length[part, kind] + u] = 0

    for c in copies():
        c.wait()

    w_at = lambda s: w[s].reshape(TILE, TILE)
    f_at = lambda s: f[s]
    x_at = lambda s: x[s]

    for q in range(CLASSES):

        def turn(p, carry, q=q):
            for u in range(TURN):
                s = q * CLASS_CAP + p * TURN + u
                w[s + HALF] = w_at(s).T.reshape(8, CHUNK, TILE)
            return carry

        lax.fori_loop(0, (total_ref[q] + TURN - 1) // TURN, turn, 0)

    def product(pairs, kind, left, left_slots, right, right_slots):
        def some(masks):
            sums, rest = [], []
            for (i, j), bits in zip(pairs, masks):
                lhs, rhs = [], []
                for _ in range(GROUPS[kind]):
                    l, bits = lowest(bits)
                    lhs.append(left(left_slots[i, l]))
                    rhs.append(right(right_slots[l, j]))
                sums.append(
                    jnp.dot(
                        jnp.concatenate(lhs, axis=1),
                        jnp.concatenate(rhs, axis=0),
                        preferred_element_type=jnp.float32,
                    )
                )
                rest.append(bits)
            return sums, rest

        sums, masks = some([near_ref[i] & near_ref[j] for i, j in pairs])
        if kind < LONG:
            return sums

        def left_over(state):
            return functools.reduce(jnp.bitwise_or, state[1]) != 0

        def more(state):
            extra, masks = some(state[1])
            return [u + v for u, v in zip(state[0], extra)], masks

        return lax.while_loop(left_over, more, (sums, masks))[0]

    def listed(part, work):
        for kind in range(LONG + 1):

            def some(g, carry, kind=kind):
                pairs = []
                for u in range(PAIRS[kind]):
                    code = todo[part, kind, g * PAIRS[kind] + u]
                    pairs.append((code >> 6, code & 63))
                work(pairs, kind)
                return carry

            lax.fori_loop(0, (length[part, kind] + PAIRS[kind] - 1) // PAIRS[kind], some, 0)

    def f_work(pairs, kind):
        for (i, j), total in zip(pairs, product(pairs, kind, w_at, slots_ref, w_at, slots_ref)):
            block = total.astype(jnp.bfloat16)
            f[slots_ref[i, j]] = block
            f[slots_ref[j, i]] = block.T

    def x_work(pairs, kind):
        for (i, j), cube in zip(pairs, product(pairs, kind, w_at, slots_ref, f_at, f_slots_ref)):
            s = x_slots_ref[i, j]
            x[s] = (1.5 * w_at(s).astype(jnp.float32) - 0.5 * cube).astype(jnp.bfloat16)

    listed(0, f_work)
    listed(1, x_work)

    for b in range(4):
        k = col * 4 + b + 1
        mine = x_slots_ref[row + 1, k]

        def some(state, k=k):
            total, bits = state
            pairs = []
            for _ in range(LAST):
                m, bits = lowest(bits)
                pairs.append((m, k))
            squares = product(pairs, LONG, x_at, x_slots_ref, x_at, x_slots_ref)
            lhs = jnp.concatenate([x[x_slots_ref[row + 1, m]] for m, _ in pairs], axis=1)
            rhs = jnp.concatenate([v.astype(jnp.bfloat16) for v in squares], axis=0)
            return total + jnp.dot(lhs, rhs, preferred_element_type=jnp.float32), bits

        bits = jnp.where(slots_ref[row + 1, k] != ZERO, near_ref[row + 1] & near_ref[k], 0)
        cube, _ = lax.while_loop(
            lambda state: state[1] != 0, some, (jnp.zeros((TILE, TILE), jnp.float32), bits)
        )
        mine = jnp.where(slots_ref[row + 1, k] != ZERO, mine, ZERO)
        out_ref[:, b * TILE : (b + 1) * TILE] = (
            1.5 * x[mine].astype(jnp.float32) - 0.5 * cube
        ).astype(jnp.bfloat16)


SMEM = pl.BlockSpec(memory_space=pltpu.SMEM)
VMEM = pl.BlockSpec(memory_space=pltpu.VMEM)
ANY = pl.BlockSpec(memory_space=pl.ANY)


def run_purify(own, other, place, table):
    bf16 = jnp.bfloat16
    return pl.pallas_call(
        purify_kernel,
        out_shape=jax.ShapeDtypeStruct((TILE, 4 * TILE), bf16),
        in_specs=[SMEM] * 9 + [ANY, ANY],
        out_specs=VMEM,
        scratch_shapes=[
            pltpu.VMEM((ZERO + 1, 8, CHUNK, TILE), bf16),
            pltpu.VMEM((ZERO + 1, TILE, TILE), bf16),
            pltpu.VMEM((ZERO + 1, TILE, TILE), bf16),
            pltpu.SMEM((2, LONG + 1, 1152), jnp.int32),
            pltpu.SMEM((2, LONG + 1), jnp.int32),
            pltpu.SemaphoreType.DMA((32,)),
        ],
        compiler_params=pltpu.CompilerParams(vmem_limit_bytes=44 * 1024 * 1024),
    )(
        place,
        table["total"],
        table["slots"],
        table["x_slots"],
        table["f_slots"],
        table["count"],
        table["near"],
        table["f_bits"],
        table["x_bits"],
        own,
        other,
    )


def sparse(density, table, row, col, rep):
    bf16 = jnp.bfloat16
    rows = lax.axis_size("row")
    pairs = [[r * 8 + c for r in (i, i + 1) for c in range(8)] for i in range(0, rows, 2)]
    got = lax.all_to_all(
        jnp.concatenate([density.reshape(8, CHUNK, 4 * TILE)] * 2),
        ("row", "col"),
        0,
        0,
        axis_index_groups=pairs,
    )
    picked = pl.pallas_call(
        pick_kernel,
        out_shape=jax.ShapeDtypeStruct((2 * PER_ROW, CHUNK, TILE), bf16),
        in_specs=[SMEM, VMEM],
        out_specs=VMEM,
    )(table["send"], got)
    everywhere = lax.all_gather(
        picked,
        "row",
        axis_index_groups=[list(range(i, rows, 2)) for i in range(2)],
    ).reshape(rows * PER_ROW, CHUNK, TILE)
    packed = pl.pallas_call(
        pack_kernel,
        out_shape=jax.ShapeDtypeStruct((CLASS_CAP, CHUNK, TILE), bf16),
        in_specs=[SMEM, VMEM],
        out_specs=VMEM,
    )(table["keep"], everywhere)
    groups = [[q * 8 + c for q in range(4) for c in range(k, 8, 2)] for k in (0, 1)]
    own = lax.all_to_all(
        jnp.broadcast_to(packed[None], (16,) + packed.shape),
        ("rep", "col"),
        0,
        0,
        axis_index_groups=groups,
    )
    other = lax.ppermute(own, "col", [(i, i ^ 1) for i in range(8)])
    place = jnp.stack([row, col, col % 2]).astype(jnp.int32)
    return run_purify(own, other, place, table)


def body(density, block_mask, tile_order):
    row, col, rep = (lax.axis_index(a) for a in ("row", "col", "rep"))
    blocks = block_mask.shape[0]
    onehot = (tile_order[:, None] == jnp.arange(blocks, dtype=jnp.int32)[None, :]).astype(
        jnp.float32
    )
    stored = exact_dot(exact_dot(onehot, block_mask), onehot.T)
    own, count, fits = owners(stored, tile_order)
    return lax.cond(
        fits,
        lambda: sparse(density, tables(stored, own, count, row, col, rep), row, col, rep),
        lambda: dense(density, stored),
    )


def solution(mesh):
    return jax.shard_map(
        body,
        mesh=mesh,
        in_specs=(P("row", "col"), P(), P()),
        out_specs=P("row", "col"),
        check_vma=False,
    )
```

```python
import functools

import jax
import jax.numpy as jnp
from jax import lax
from jax.experimental import pallas as pl
from jax.experimental.pallas import tpu as pltpu
from jax.sharding import PartitionSpec as P

TILE = 128
STEPS = 2
CHUNK = 16
CLASSES = 4
PER_ROW = 3
CLASS_CAP = 40
HALF = CLASSES * CLASS_CAP
GROUPS = (4, 8, 8)
LONG = len(GROUPS) - 1
PAIRS = (8, 4, 1)
LAST = 3
TURN = 10
ZERO = 2 * HALF


def dense(density, stored):
    height, breadth = density.shape
    layer_count = lax.axis_size("rep")
    layer_index = lax.axis_index("rep")
    row_count = lax.axis_size("row")
    row_index = lax.axis_index("row")
    col_index = lax.axis_index("col")
    block_rows = height // TILE
    block_cols = breadth // TILE
    local_blocks = lax.dynamic_slice(
        stored, (row_index * block_rows, col_index * block_cols), (block_rows, block_cols)
    )
    retain = jnp.broadcast_to(
        local_blocks[:, None, :, None], (block_rows, TILE, block_cols, TILE)
    ).reshape(height, breadth)

    def multiply(gathered_panel, operand):
        sub_rows = height // layer_count
        shaped = gathered_panel.reshape(height, row_count, layer_count, sub_rows)
        selected = lax.dynamic_index_in_dim(shaped, layer_index, 2, keepdims=False).reshape(
            height, row_count * sub_rows
        )
        portion_rows = lax.dynamic_slice_in_dim(operand, layer_index * sub_rows, sub_rows, 0)
        partial_sum = jnp.dot(
            selected,
            lax.all_gather(portion_rows, "row", axis=0, tiled=True),
            preferred_element_type=jnp.float32,
        )
        return lax.psum(partial_sum, "rep")

    matrix = density
    for step_number in range(STEPS):
        gathered_panel = lax.all_gather(matrix, "col", axis=1, tiled=True)
        square = multiply(gathered_panel, matrix)
        filtered = (retain * square).astype(jnp.bfloat16)
        cube = multiply(gathered_panel, filtered)
        matrix = (retain * (1.5 * matrix.astype(jnp.float32) - 0.5 * cube)).astype(jnp.bfloat16)
    return matrix


def exact_dot(a, b):
    return jnp.dot(
        a.astype(jnp.bfloat16), b.astype(jnp.bfloat16), preferred_element_type=jnp.float32
    )


def owners(stored, tile_order):
    nb = stored.shape[0]
    index = jnp.arange(nb, dtype=jnp.int32)
    apart = (tile_order[None, :] - tile_order[:, None]) % nb
    mine = (apart < nb // 2) | ((apart == nb // 2) & (tile_order[:, None] < nb // 2))
    own = jnp.where(mine, stored, 0)
    owned = jnp.sum(own, axis=1).astype(jnp.int32)
    classes = jnp.arange(CLASSES, dtype=jnp.int32)
    first = (classes[:, None] - index[None, :]) % CLASSES
    count = (owned[None, :] - first + CLASSES - 1) // CLASSES
    total = jnp.sum(count, axis=1)
    over = jnp.concatenate([owned - PER_ROW * CLASSES, total - CLASS_CAP])
    return own, count, jnp.max(over) <= 0


def tables(stored, own, count, row, col, rep):
    nb = stored.shape[0]
    kept = stored > 0.5
    index = jnp.arange(nb, dtype=jnp.int32)
    before = (index[:, None] < index[None, :]).astype(jnp.float32)
    rank = exact_dot(own, before).astype(jnp.int32)
    total = jnp.sum(count, axis=1)
    base = jnp.sum(
        jnp.where(index[None, None, :] < index[None, :, None], count[:, None, :], 0), axis=2
    )
    pair = row - row % 2
    pair_own = lax.dynamic_slice_in_dim(own, pair, 2, 0) > 0.5
    pair_rank = lax.dynamic_slice_in_dim(rank, pair, 2, 0)
    turn = (rep - pair - jnp.arange(2, dtype=jnp.int32)) % CLASSES
    wanted = jnp.arange(PER_ROW, dtype=jnp.int32)[None, :] * CLASSES + turn[:, None]
    hit = pair_own[:, None, :] & (pair_rank[:, None, :] == wanted[:, :, None])
    send = jnp.sum(jnp.where(hit, index[None, None, :] + 1, 0), axis=2) - 1
    send = send.reshape(2 * PER_ROW)
    my_base = lax.dynamic_index_in_dim(base, rep, 0, keepdims=False)
    my_count = lax.dynamic_index_in_dim(count, rep, 0, keepdims=False)
    place = jnp.arange(CLASS_CAP, dtype=jnp.int32)[:, None]
    inside = (place >= my_base[None, :]) & (place < (my_base + my_count)[None, :])
    keep = (
        jnp.sum(
            jnp.where(inside, index[None, :] * PER_ROW + place - my_base[None, :] + 1, 0), axis=1
        )
        - 1
    )
    which = (rank + index[:, None]) % CLASSES
    start = jnp.zeros_like(rank)
    for c in range(CLASSES):
        start = jnp.where(which == c, base[c][:, None] + c * CLASS_CAP, start)
    slot = start + rank // CLASSES
    slots = jnp.where(own > 0.5, slot, jnp.where(kept, slot.T + HALF, ZERO))
    a = stored
    er = lax.dynamic_index_in_dim(stored, row, 0, keepdims=False)
    k_set = er * ((index // (nb // 8)) == col)
    through = exact_dot(a * k_set[None, :], a)
    need_x = kept & ((k_set[None, :] > 0.5) | ((er[:, None] > 0.5) & (through > 0.5)))
    need_f = exact_dot(a, need_x) > 0.5
    need_f = kept & (need_f | need_f.T)
    x_slots = jnp.where(need_x, slots, ZERO)
    f_slots = jnp.where(need_f, slots, ZERO)
    pad = lambda t: jnp.pad(t, ((1, 0), (1, 0)), constant_values=ZERO)
    powers = jnp.left_shift(jnp.int32(1), index)
    bits = lambda t: jnp.pad(jnp.sum(jnp.where(t, powers[:, None], 0), axis=0), (1, 0))
    common = exact_dot(a, a)
    kinds = sum((common > g).astype(jnp.int32) for g in GROUPS[:LONG])
    return dict(
        send=send,
        keep=keep,
        slots=pad(slots),
        x_slots=pad(x_slots),
        f_slots=pad(f_slots),
        count=jnp.pad(kinds, ((1, 0), (1, 0))),
        near=bits(kept),
        f_bits=bits(need_f & (own > 0.5)),
        x_bits=bits(need_x),
        total=total,
    )


def pick_kernel(send_ref, got_ref, out_ref):
    for t in range(2 * PER_ROW):
        b = send_ref[t]
        at = jnp.maximum(b, 0)
        tile = got_ref[t // PER_ROW * 8 + at // 4, :, pl.ds(pl.multiple_of((at % 4) * TILE, TILE), TILE)]
        out_ref[t] = jnp.where(b >= 0, tile, jnp.zeros_like(tile))


def pack_kernel(keep_ref, all_ref, out_ref):
    def one(p, carry):
        e = keep_ref[p]
        tile = all_ref[jnp.maximum(e, 0)]
        tile = jnp.where(e >= 0, tile, jnp.zeros_like(tile))
        for d in range(out_ref.shape[0]):
            out_ref[d, p] = tile
        return carry

    lax.fori_loop(0, CLASS_CAP, one, 0, unroll=4)


def purify_kernel(
    place_ref,
    total_ref,
    slots_ref,
    x_slots_ref,
    f_slots_ref,
    count_ref,
    near_ref,
    f_bits_ref,
    x_bits_ref,
    own_ref,
    other_ref,
    out_ref,
    w,
    f,
    x,
    todo,
    length,
    sems,
):
    row, col, core = place_ref[0], place_ref[1], place_ref[2]
    nb = 32

    def copies():
        for part, (ref, half) in enumerate(((own_ref, core), (other_ref, 1 - core))):
            for q in range(CLASSES):
                for y in range(4):
                    yield pltpu.make_async_copy(
                        ref.at[q * 4 + y],
                        w.at[pl.ds(q * CLASS_CAP, CLASS_CAP), 2 * y + half],
                        sems.at[part * 16 + q * 4 + y],
                    )

    for c in copies():
        c.start()
    zero = jnp.zeros((TILE, TILE), jnp.bfloat16)
    w[ZERO] = zero.reshape(8, CHUNK, TILE)
    f[ZERO] = zero
    x[ZERO] = zero
    def lowest(bits):
        return 32 - lax.clz(bits & -bits), bits & (bits - 1)

    for part, bits_ref in enumerate((f_bits_ref, x_bits_ref)):
        for kind in range(LONG + 1):
            length[part, kind] = 0

        def column(j, carry, part=part, bits_ref=bits_ref):
            def add(bits):
                i, bits = lowest(bits)
                kind = count_ref[i, j]
                at = length[part, kind]
                todo[part, kind, at] = i * 64 + j
                length[part, kind] = at + 1
                return bits

            lax.while_loop(lambda bits: bits != 0, add, bits_ref[j])
            return carry

        lax.fori_loop(1, nb + 1, column, 0)
        for kind in range(LONG + 1):
            for u in range(PAIRS[kind]):
                todo[part, kind, length[part, kind] + u] = 0

    for c in copies():
        c.wait()

    w_at = lambda s: w[s].reshape(TILE, TILE)
    f_at = lambda s: f[s]
    x_at = lambda s: x[s]

    for q in range(CLASSES):

        def turn(p, carry, q=q):
            for u in range(TURN):
                s = q * CLASS_CAP + p * TURN + u
                w[s + HALF] = w_at(s).T.reshape(8, CHUNK, TILE)
            return carry

        lax.fori_loop(0, (total_ref[q] + TURN - 1) // TURN, turn, 0)

    def product(pairs, kind, left, left_slots, right, right_slots):
        def some(masks):
            sums, rest = [], []
            for (i, j), bits in zip(pairs, masks):
                lhs, rhs = [], []
                for _ in range(GROUPS[kind]):
                    l, bits = lowest(bits)
                    lhs.append(left(left_slots[i, l]))
                    rhs.append(right(right_slots[l, j]))
                sums.append(
                    jnp.dot(
                        jnp.concatenate(lhs, axis=1),
                        jnp.concatenate(rhs, axis=0),
                        preferred_element_type=jnp.float32,
                    )
                )
                rest.append(bits)
            return sums, rest

        sums, masks = some([near_ref[i] & near_ref[j] for i, j in pairs])
        if kind < LONG:
            return sums

        def left_over(state):
            return functools.reduce(jnp.bitwise_or, state[1]) != 0

        def more(state):
            extra, masks = some(state[1])
            return [u + v for u, v in zip(state[0], extra)], masks

        return lax.while_loop(left_over, more, (sums, masks))[0]

    def listed(part, work):
        for kind in range(LONG + 1):

            def some(g, carry, kind=kind):
                pairs = []
                for u in range(PAIRS[kind]):
                    code = todo[part, kind, g * PAIRS[kind] + u]
                    pairs.append((code >> 6, code & 63))
                work(pairs, kind)
                return carry

            lax.fori_loop(0, (length[part, kind] + PAIRS[kind] - 1) // PAIRS[kind], some, 0)

    def f_work(pairs, kind):
        for (i, j), total in zip(pairs, product(pairs, kind, w_at, slots_ref, w_at, slots_ref)):
            block = total.astype(jnp.bfloat16)
            f[slots_ref[i, j]] = block
            f[slots_ref[j, i]] = block.T

    def x_work(pairs, kind):
        for (i, j), cube in zip(pairs, product(pairs, kind, w_at, slots_ref, f_at, f_slots_ref)):
            s = x_slots_ref[i, j]
            x[s] = (1.5 * w_at(s).astype(jnp.float32) - 0.5 * cube).astype(jnp.bfloat16)

    listed(0, f_work)
    listed(1, x_work)

    for b in range(4):
        k = col * 4 + b + 1
        mine = x_slots_ref[row + 1, k]

        def some(state, k=k):
            total, bits = state
            pairs = []
            for _ in range(LAST):
                m, bits = lowest(bits)
                pairs.append((m, k))
            squares = product(pairs, LONG, x_at, x_slots_ref, x_at, x_slots_ref)
            lhs = jnp.concatenate([x[x_slots_ref[row + 1, m]] for m, _ in pairs], axis=1)
            rhs = jnp.concatenate([v.astype(jnp.bfloat16) for v in squares], axis=0)
            return total + jnp.dot(lhs, rhs, preferred_element_type=jnp.float32), bits

        bits = jnp.where(slots_ref[row + 1, k] != ZERO, near_ref[row + 1] & near_ref[k], 0)
        cube, _ = lax.while_loop(
            lambda state: state[1] != 0, some, (jnp.zeros((TILE, TILE), jnp.float32), bits)
        )
        mine = jnp.where(slots_ref[row + 1, k] != ZERO, mine, ZERO)
        out_ref[:, b * TILE : (b + 1) * TILE] = (
            1.5 * x[mine].astype(jnp.float32) - 0.5 * cube
        ).astype(jnp.bfloat16)


SMEM = pl.BlockSpec(memory_space=pltpu.SMEM)
VMEM = pl.BlockSpec(memory_space=pltpu.VMEM)
ANY = pl.BlockSpec(memory_space=pl.ANY)


def run_purify(own, other, place, table):
    bf16 = jnp.bfloat16
    return pl.pallas_call(
        purify_kernel,
        out_shape=jax.ShapeDtypeStruct((TILE, 4 * TILE), bf16),
        in_specs=[SMEM] * 9 + [ANY, ANY],
        out_specs=VMEM,
        scratch_shapes=[
            pltpu.VMEM((ZERO + 1, 8, CHUNK, TILE), bf16),
            pltpu.VMEM((ZERO + 1, TILE, TILE), bf16),
            pltpu.VMEM((ZERO + 1, TILE, TILE), bf16),
            pltpu.SMEM((2, LONG + 1, 1152), jnp.int32),
            pltpu.SMEM((2, LONG + 1), jnp.int32),
            pltpu.SemaphoreType.DMA((32,)),
        ],
        compiler_params=pltpu.CompilerParams(vmem_limit_bytes=44 * 1024 * 1024),
    )(
        place,
        table["total"],
        table["slots"],
        table["x_slots"],
        table["f_slots"],
        table["count"],
        table["near"],
        table["f_bits"],
        table["x_bits"],
        own,
        other,
    )


def sparse(density, table, row, col, rep):
    bf16 = jnp.bfloat16
    rows = lax.axis_size("row")
    pairs = [[r * 8 + c for r in (i, i + 1) for c in range(8)] for i in range(0, rows, 2)]
    got = lax.all_to_all(
        jnp.broadcast_to(density.reshape(1, 8, CHUNK, 4 * TILE), (2, 8, CHUNK, 4 * TILE)).reshape(
            16, CHUNK, 4 * TILE
        ),
        ("row", "col"),
        0,
        0,
        axis_index_groups=pairs,
    )
    picked = pl.pallas_call(
        pick_kernel,
        out_shape=jax.ShapeDtypeStruct((2 * PER_ROW, CHUNK, TILE), bf16),
        in_specs=[SMEM, VMEM],
        out_specs=VMEM,
    )(table["send"], got)
    everywhere = lax.all_gather(
        picked,
        "row",
        axis_index_groups=[list(range(i, rows, 2)) for i in range(2)],
    ).reshape(rows * PER_ROW, CHUNK, TILE)
    packed = pl.pallas_call(
        pack_kernel,
        out_shape=jax.ShapeDtypeStruct((16, CLASS_CAP, CHUNK, TILE), bf16),
        in_specs=[SMEM, VMEM],
        out_specs=VMEM,
    )(table["keep"], everywhere)
    groups = [[q * 8 + c for q in range(4) for c in range(k, 8, 2)] for k in (0, 1)]
    own = lax.all_to_all(packed, ("rep", "col"), 0, 0, axis_index_groups=groups)
    other = lax.ppermute(own, "col", [(i, i ^ 1) for i in range(8)])
    place = jnp.stack([row, col, col % 2]).astype(jnp.int32)
    return run_purify(own, other, place, table)


def body(density, block_mask, tile_order):
    row, col, rep = (lax.axis_index(a) for a in ("row", "col", "rep"))
    blocks = block_mask.shape[0]
    onehot = (tile_order[:, None] == jnp.arange(blocks, dtype=jnp.int32)[None, :]).astype(
        jnp.float32
    )
    stored = exact_dot(exact_dot(onehot, block_mask), onehot.T)
    own, count, fits = owners(stored, tile_order)
    return lax.cond(
        fits,
        lambda: sparse(density, tables(stored, own, count, row, col, rep), row, col, rep),
        lambda: dense(density, stored),
    )


def solution(mesh):
    return jax.shard_map(
        body,
        mesh=mesh,
        in_specs=(P("row", "col"), P(), P()),
        out_specs=P("row", "col"),
        check_vma=False,
    )
```
